32 devices in a mesh: dp: 4 (over y, x), ctx: 8 (over z, core).
Axes of the slice: x: 2, y: 2, z: 4, core: 2. Of those that a mesh axis runs over, the one named last changes fastest.
Arguments:
- queries: bfloat16 [4, 1024, 1280], P('dp', 'ctx'), may hold values from -16 to 16
- keys: bfloat16 [4, 1024, 1280], P('dp', 'ctx'), may hold values from -16 to 16
- values: bfloat16 [4, 1024, 1280], P('dp', 'ctx'), may hold values from -6 to 6
- seg_lengths: int32 [4, 8], P('dp'), may hold values from 1 to 768, 1024 in all within a row
- out_grad: bfloat16 [4, 1024, 2560], P('dp', 'ctx'), may hold values from -6 to 6
- w_out: bfloat16 [1280, 2560], P('dp'), may hold values from -0.15625 to 0.15625
Outputs:
- attended: bfloat16 [4, 1024, 2560], P('dp', 'ctx')
- query_grad: bfloat16 [4, 1024, 1280], P('dp', 'ctx')
- key_grad: bfloat16 [4, 1024, 1280], P('dp', 'ctx')
- value_grad: bfloat16 [4, 1024, 1280], P('dp', 'ctx')
- w_out_grad: float32 [1280, 2560], P('dp')
The draws below stay inside these ranges and needn't reach their ends.
Inputs may be any that keep to these rules, and one draw needn't show every extreme that they name: `seg_lengths`: each record's lengths sum to 1024; the longest of each record is exactly 768.
All inputs are finite; a program needn't handle non-finite values.
Results may differ from the reference program's by a relative error of at most 0.027.
Values may be sent and summed in bfloat16 or wider, within the bound.
A program may use at most 192 MiB of HBM per device.

```python
import math
import jax
import jax.numpy as jnp
import numpy as np
from jax import lax

D = 2560
HEADS = 10
HD = 128
NSEG = 8
INNER = 1280
SEQ = 1024
SEG_MOST = 768
BATCH = 4


def base_rows(key, spread_low, spread_high, factor):
    row_scale = jnp.exp(jax.random.uniform(jax.random.fold_in(key, 31), (BATCH, SEQ, HEADS, 1), minval=math.log(spread_low), maxval=math.log(spread_high)))
    entries = jnp.clip(jax.random.normal(jax.random.fold_in(key, 32), (BATCH, SEQ, HEADS, HD)), -4.0, 4.0)
    return factor * row_scale * entries


def draw_queries(key, part):
    base = base_rows(jax.random.fold_in(key, 41), 0.5, 2.0, 0.8)
    result = base
    return result.reshape(BATCH, SEQ, HEADS * HD).astype(jnp.bfloat16)


def draw_keys(key, part):
    base = base_rows(jax.random.fold_in(key, 42), 0.3, 3.0, 1.0)
    result = base
    return result.reshape(BATCH, SEQ, HEADS * HD).astype(jnp.bfloat16)


def steps_of(key, shape, split, least, largest):
    level = 1.0
    for dim, parts in split:
        draws = jax.random.uniform(jax.random.fold_in(jax.random.fold_in(key, 6), dim), (parts,), jnp.float32, least / len(split), largest / len(split))
        level = level * jnp.repeat(jnp.exp(draws), shape[dim] // parts).reshape((-1,) + (1,) * (len(shape) - 1 - dim))
    return level


def length_profile(number_of, total, bound, lean):
    weights = [(1 << 20) // math.isqrt(grade ** lean) + 1 for grade in range(2, number_of + 1)]
    surplus, holding = total - bound - (number_of - 1), [1] * (number_of - 1)
    while surplus > 0:
        movable = [i for i in range(number_of - 1) if holding[i] < bound]
        whole, budget = sum([weights[i] for i in movable]), surplus
        for i in movable:
            more = min(bound - holding[i], max(1, budget * weights[i] // whole), surplus)
            holding[i] = holding[i] + more
            surplus = surplus - more
    return np.array([bound] + holding)


def uneven(rng, count, total, limit, lean):
    if count == 2:
        one = jax.random.randint(rng, (), max(1, total - limit), min(limit, total - 1) + 1)
        return jnp.stack([one, total - one])
    tallies = jnp.asarray(length_profile(count, total, limit, lean), jnp.int32)
    pairs = (count - 1) // 2
    giver, sink = tallies[1:1 + 2 * pairs:2], tallies[2:2 + 2 * pairs:2]
    slack = jnp.minimum(giver - 1, limit - sink)
    shifted = jax.random.randint(jax.random.fold_in(rng, 1), (pairs,), 0, 1 << 20) % (slack + 1)
    tallies = tallies.at[1:1 + 2 * pairs:2].set(giver - shifted).at[2:2 + 2 * pairs:2].set(sink + shifted)
    return tallies[jax.random.permutation(jax.random.fold_in(rng, 2), count)]


def normal_values(rng, extent, scale, reach, shards=(), kind=jnp.bfloat16):
    array = jax.random.normal(rng, extent, jnp.float32) * scale
    if len(shards) > 0:
        array = steps_of(rng, extent, shards, -0.22, 0.18) * array
    return jnp.clip(array, min=-reach, max=reach).astype(kind)


def setup_inputs(seed: int = 0) -> dict:
    key_list = jax.random.split(jax.random.key(seed), 7)
    return {
        "queries": draw_queries(jax.random.fold_in(key_list[6], 71), 0),
        "keys": draw_keys(jax.random.fold_in(key_list[6], 71), 0),
        "values": normal_values(key_list[2], (BATCH, SEQ, INNER), 1.0, 6.0, ((0, 4), (1, 8))),
        "seg_lengths": jax.vmap(lambda own: uneven(own, NSEG, SEQ, SEG_MOST, 2))(jax.random.split(key_list[3], BATCH)).reshape((BATCH, NSEG)).astype(jnp.int32),
        "out_grad": normal_values(key_list[4], (BATCH, SEQ, D), 1.0, 6.0, ((0, 4), (1, 8))),
        "w_out": normal_values(key_list[5], (INNER, D), INNER ** -0.5, 0.15625, ((0, 4),)),
    }


MASKED_SCORE = -1e+30

def segment_ids(length_row):
    segment_ends = jnp.cumsum(length_row).astype(jnp.int32)
    positions = jnp.arange(SEQ, dtype=jnp.int32)
    return lax.optimization_barrier(jnp.sum((segment_ends[None, :] <= positions[:, None]).astype(jnp.int32), axis=1))

def one_head(operands):
    query_head, key_head, value_head, grad_head, segments = operands
    score_scale = 1.0 / math.sqrt(HD)
    block_rows = min(SEQ, 512)
    block_count = SEQ // block_rows

    def block_scores(first_row):
        query_block = lax.dynamic_slice_in_dim(query_head, first_row, block_rows, 0)
        scores = jnp.dot(query_block, key_head.T, preferred_element_type=jnp.float32) * score_scale
        query_segments = lax.dynamic_slice_in_dim(segments, first_row, block_rows, 0)
        return (scores, query_segments[:, None] == segments[None, :])

    def forward(block_index):
        first_row = block_index * block_rows
        scores, same_segment = block_scores(first_row)
        row_max = lax.optimization_barrier(jnp.max(jnp.where(same_segment, scores, MASKED_SCORE), axis=1))
        row_sum = lax.optimization_barrier(jnp.sum(jnp.where(same_segment, jnp.exp(scores - row_max[:, None]), 0.0), axis=1))
        log_norm = row_max + jnp.log(row_sum)
        probs = jnp.where(same_segment, jnp.exp(scores - log_norm[:, None]), 0.0)
        attention = jnp.dot(probs.astype(jnp.bfloat16), value_head, preferred_element_type=jnp.float32)
        return (attention.astype(jnp.bfloat16), log_norm)
    attention, log_norm = lax.map(forward, jnp.arange(block_count, dtype=jnp.int32))
    attention = attention.reshape(SEQ, HD)
    log_norm = log_norm.reshape(SEQ)
    grad_dot = lax.optimization_barrier(jnp.sum(grad_head.astype(jnp.float32) * attention.astype(jnp.float32), axis=1))

    def backward(carried, block_index):
        key_sum, value_sum = carried
        first_row = block_index * block_rows
        scores, same_segment = block_scores(first_row)
        query_block = lax.dynamic_slice_in_dim(query_head, first_row, block_rows, 0)
        grad_block = lax.dynamic_slice_in_dim(grad_head, first_row, block_rows, 0)
        norm_block = lax.dynamic_slice_in_dim(log_norm, first_row, block_rows, 0)
        dot_block = lax.dynamic_slice_in_dim(grad_dot, first_row, block_rows, 0)
        probs = jnp.where(same_segment, jnp.exp(scores - norm_block[:, None]), 0.0)
        probs_b = probs.astype(jnp.bfloat16)
        dprob = jnp.dot(grad_block, value_head.T, preferred_element_type=jnp.float32)
        dscore_b = (probs * (dprob - dot_block[:, None])).astype(jnp.bfloat16)
        query_part = jnp.dot(dscore_b, key_head, preferred_element_type=jnp.float32) * score_scale
        key_sum = key_sum + jnp.dot(dscore_b.T, query_block, preferred_element_type=jnp.float32)
        value_sum = value_sum + jnp.dot(probs_b.T, grad_block, preferred_element_type=jnp.float32)
        return ((key_sum, value_sum), query_part.astype(jnp.bfloat16))
    zeros = jnp.zeros((SEQ, HD), jnp.float32)
    (key_sum, value_sum), query_part = lax.scan(backward, (zeros, zeros), jnp.arange(block_count, dtype=jnp.int32))
    key_part = (key_sum * score_scale).astype(jnp.bfloat16)
    return (attention, query_part.reshape(SEQ, HD), key_part, value_sum.astype(jnp.bfloat16))

def split_heads(matrix):
    return matrix.reshape(BATCH, SEQ, HEADS, HD).transpose(0, 2, 1, 3).reshape(BATCH * HEADS, SEQ, HD)

def merge_heads(matrix):
    return matrix.reshape(BATCH, HEADS, SEQ, HD).transpose(0, 2, 1, 3).reshape(BATCH, SEQ, INNER)

def reference(queries, keys, values, seg_lengths, out_grad, w_out):
    flat_grad = out_grad.reshape(BATCH * SEQ, D)
    attn_grad = jnp.dot(flat_grad, w_out.T, preferred_element_type=jnp.float32).astype(jnp.bfloat16)
    attn_grad = attn_grad.reshape(BATCH, SEQ, INNER)
    segments = jax.vmap(segment_ids)(seg_lengths)
    segments = jnp.repeat(segments, HEADS, axis=0)
    operands = (split_heads(queries), split_heads(keys), split_heads(values), split_heads(attn_grad), segments)
    attention, query_part, key_part, value_part = lax.map(one_head, operands)
    attention = merge_heads(attention)
    flat_attention = attention.reshape(BATCH * SEQ, INNER)
    attended = jnp.dot(flat_attention, w_out, preferred_element_type=jnp.float32).astype(jnp.bfloat16)
    w_out_grad = jnp.dot(flat_attention.T, flat_grad, preferred_element_type=jnp.float32)
    return (attended.reshape(BATCH, SEQ, D), merge_heads(query_part), merge_heads(key_part), merge_heads(value_part), w_out_grad)
```

```python
import functools
import math

import jax
import jax.numpy as jnp
from jax import lax
from jax.experimental import pallas as pl
from jax.experimental.pallas import tpu as pltpu
from jax.sharding import PartitionSpec as P

HEADS = 10
HD = 128
MASKED_SCORE = -1e30
MESH = pl.DeviceIdType.MESH
BF16 = jnp.bfloat16
F32 = jnp.float32
VMEM_BYTES = 56 * 1024 * 1024


def owner_of(head, n):
    slot, place = divmod(head, n)
    if slot and 2 * place + 2 < n:
        place = 2 * place + 2
    return place, slot


def head_in_slot(me, slot, n):
    if slot == 0:
        return me, me < HEADS
    head, valid = 0, False
    for h in range(slot * n, min(HEADS, (slot + 1) * n)):
        place = owner_of(h, n)[0]
        head = jnp.where(me == place, h, head)
        valid = jnp.logical_or(valid, me == place)
    return head, valid


def dot_nt(a, b):
    return lax.dot_general(a, b, (((1,), (1,)), ((), ())), preferred_element_type=F32)


def dot_tn(a, b):
    return lax.dot_general(a, b, (((0,), (0,)), ((), ())), preferred_element_type=F32)


def dot_nn(a, b):
    return jnp.dot(a, b, preferred_element_type=F32)


def remote(src, dst, send, recv, dp, ctx):
    return pltpu.make_async_remote_copy(
        src_ref=src, dst_ref=dst, send_sem=send, recv_sem=recv, device_id=(dp, ctx), device_id_type=MESH
    )


def greet(n, ndp):
    me, dp = lax.axis_index("ctx"), lax.axis_index("dp")
    barrier = pltpu.get_barrier_semaphore()
    for step in range(1, n):
        pl.semaphore_signal(barrier, inc=1, device_id=(dp, lax.rem(me + step, n)), device_id_type=MESH)
    for step in range(1, ndp):
        pl.semaphore_signal(barrier, inc=1, device_id=(lax.rem(dp + step, ndp), me), device_id_type=MESH)
    pl.semaphore_wait(barrier, n - 1 + ndp - 1)


def scatter_kernel(
    n, ndp, q_ref, k_ref, v_ref, og_ref, w_ref, heads_ref, full_ref, grad_ref,
    send_sem, recv_sem, wsend, wrecv, fsend, frecv,
):
    me, dp = lax.axis_index("ctx"), lax.axis_index("dp")
    core = lax.rem(me, 2)
    sibling = me + 1 - 2 * core
    rows = q_ref.shape[0]
    wrows = w_ref.shape[0]
    half = wrows // 2
    greet(n, ndp)
    my_rows = pl.ds(pl.multiple_of(me * rows, rows), rows)

    def weight_rows(owner, which):
        return pl.ds(pl.multiple_of(owner * wrows + which * half, 16), half)

    weight_copies = []
    for step in range(1, ndp):
        copy = remote(
            w_ref.at[pl.ds(pl.multiple_of(core * half, 16), half)],
            full_ref.at[weight_rows(dp, core)],
            wsend.at[step], wrecv.at[step], lax.rem(dp + step, ndp), me,
        )
        copy.start()
        weight_copies.append(copy)

    def send_head(tensor, source, head, start):
        place, slot = owner_of(head, n)
        columns = pl.ds(head * HD, HD)
        copy = remote(
            source.at[:, columns], heads_ref.at[slot, tensor, my_rows],
            send_sem.at[tensor, head], recv_sem.at[slot, tensor], dp, place,
        )

        @pl.when(me != place)
        def _():
            if start:
                copy.start()
            else:
                copy.wait_send()

        if start:
            @pl.when(me == place)
            def _():
                heads_ref[slot, tensor, my_rows, :] = source[:, columns]

    for tensor, source in enumerate((q_ref, k_ref, v_ref)):
        for head in range(HEADS):
            send_head(tensor, source, head, True)

    full_ref[pl.ds(pl.multiple_of(dp * wrows, 16), wrows), :] = w_ref[...]
    passes = []
    for step in range(1, ndp):
        weight_copies[step - 1].wait_recv()
        source = lax.rem(dp - step + ndp, ndp)
        block = full_ref.at[weight_rows(source, core)]
        copy = remote(block, block, fsend.at[step], frecv.at[step], dp, sibling)
        copy.start()
        passes.append(copy)
    for copy in passes:
        copy.wait_recv()
    for head in range(HEADS):
        columns = pl.ds(head * HD, HD)
        grad_ref[:, columns] = dot_nt(og_ref[...], full_ref[columns, :]).astype(BF16)
        send_head(3, grad_ref, head, True)

    for tensor, source in enumerate((q_ref, k_ref, v_ref, grad_ref)):
        for head in range(HEADS):
            send_head(tensor, source, head, False)
    for copy in weight_copies + passes:
        copy.wait_send()
    slots = heads_ref.shape[0]
    for slot in range(slots):
        @pl.when(head_in_slot(me, slot, n)[1])
        def _():
            for tensor in range(4):
                waited = heads_ref.at[slot, tensor, pl.ds(0, rows * (n - 1))]
                pltpu.make_async_copy(waited, waited, recv_sem.at[slot, tensor]).wait()


def attention_kernel(n, block, heads_ref, seg_col_ref, seg_row_ref, out_ref, key_sum, value_sum):
    me = lax.axis_index("ctx")
    scale = 1.0 / math.sqrt(HD)
    slots, _, seq, _ = heads_ref.shape
    for slot in range(slots):
        @pl.when(head_in_slot(me, slot, n)[1])
        def _():
            key_sum[...] = jnp.zeros_like(key_sum)
            value_sum[...] = jnp.zeros_like(value_sum)

            @pl.loop(0, seq // block)
            def _(index):
                rows = pl.ds(pl.multiple_of(index * block, block), block)
                query, grad = heads_ref[slot, 0, rows, :], heads_ref[slot, 3, rows, :]
                key, value = heads_ref[slot, 1], heads_ref[slot, 2]
                seen = seg_col_ref[rows, :] == seg_row_ref[...]
                scores = jnp.where(seen, dot_nt(query, key) * scale, MASKED_SCORE)
                top = jnp.max(scores, axis=1, keepdims=True)
                shifted = jnp.exp(scores - top)
                probs = shifted * (1.0 / jnp.sum(shifted, axis=1, keepdims=True))
                probs_b = probs.astype(BF16)
                attention = dot_nn(probs_b, value).astype(BF16)
                out_ref[slot, 0, rows, :] = attention
                grad_dot = jnp.sum(grad.astype(F32) * attention.astype(F32), axis=1, keepdims=True)
                dscore = (probs * (dot_nt(grad, value) - grad_dot)).astype(BF16)
                out_ref[slot, 1, rows, :] = (dot_nn(dscore, key) * scale).astype(BF16)
                key_sum[...] += dot_tn(dscore, query)
                value_sum[...] += dot_tn(probs_b, grad)

            out_ref[slot, 2] = (key_sum[...] * scale).astype(BF16)
            out_ref[slot, 3] = value_sum[...].astype(BF16)


def home_kernel(
    n, ndp, parts, heads_ref, full_ref, og_ref,
    attended_ref, qg_ref, kg_ref, vg_ref, wg_ref,
    att_ref, att_t, xsend_buf, xrecv_buf, csum, rbuf, hsum, zbuf, final,
    hsend, hrecv, xsend, xrecv, rsend, rrecv, zsend, zrecv, bsend, brecv, fsend, frecv,
):
    me, dp = lax.axis_index("ctx"), lax.axis_index("dp")
    core = lax.rem(me, 2)
    chip = me // 2
    sibling = me + 1 - 2 * core
    slots, _, seq, _ = heads_ref.shape
    rows = seq // n
    width = og_ref.shape[1]
    half = csum.shape[1]
    wide = width // parts
    tile = 512
    greet(n, ndp)
    targets = (att_ref, qg_ref, kg_ref, vg_ref)

    def home_copy(slot, tensor, step):
        head, valid = head_in_slot(me, slot, n)
        other = lax.rem(me + step, n)
        columns = pl.ds(pl.multiple_of(head * HD, HD), HD)
        source = heads_ref.at[slot, tensor, pl.ds(pl.multiple_of(other * rows, rows), rows)]
        return valid, remote(
            source, targets[tensor].at[:, columns],
            hsend.at[tensor, slot, step], hrecv.at[tensor, head], dp, other,
        )

    def send_home(tensor):
        for slot in range(slots):
            head, valid = head_in_slot(me, slot, n)

            @pl.when(valid)
            def _():
                for step in range(1, n):
                    home_copy(slot, tensor, step)[1].start()
                columns = pl.ds(pl.multiple_of(head * HD, HD), HD)
                mine = pl.ds(pl.multiple_of(me * rows, rows), rows)
                targets[tensor][:, columns] = heads_ref[slot, tensor, mine, :]

    def receive_home(tensor):
        for head in range(HEADS):
            place, _ = owner_of(head, n)

            @pl.when(me != place)
            def _():
                block = targets[tensor].at[:, pl.ds(head * HD, HD)]
                remote(block, block, hsend.at[tensor, 0, 0], hrecv.at[tensor, head], dp, place).wait_recv()

    for tensor in range(4):
        send_home(tensor)
    receive_home(0)

    att_t[...] = att_ref[...].T

    def share(owner, which):
        return pl.multiple_of(owner * 2 * half + which * half, 16)

    sib_copies = []
    for step in range(ndp):
        owner = lax.rem(dp + step + 1, ndp)
        left = att_t[pl.ds(share(owner, 1 - core), half), :]

        @pl.loop(0, width // tile)
        def _(index):
            columns = pl.ds(pl.multiple_of(index * tile, tile), tile)
            xsend_buf[step, :, columns] = dot_nn(left, og_ref[:, columns]).astype(BF16)

        copy = remote(xsend_buf.at[step], xrecv_buf.at[step], xsend.at[step], xrecv.at[step], dp, sibling)
        copy.start()
        sib_copies.append(copy)
    dp_copies = []
    for step in range(ndp):
        owner = lax.rem(dp + step + 1, ndp)
        left = att_t[pl.ds(share(owner, core), half), :]
        sib_copies[step].wait_recv()

        @pl.loop(0, width // tile)
        def _(index):
            columns = pl.ds(pl.multiple_of(index * tile, tile), tile)
            total = dot_nn(left, og_ref[:, columns]) + xrecv_buf[step, :, columns].astype(F32)
            csum[step, :, columns] = total.astype(BF16)

        if step < ndp - 1:
            copy = remote(csum.at[step], rbuf.at[step], rsend.at[step], rrecv.at[step], owner, me)
            copy.start()
            dp_copies.append(copy)

    @pl.loop(0, width // tile)
    def _(index):
        columns = pl.ds(pl.multiple_of(index * tile, tile), tile)
        attended_ref[:, columns] = dot_nn(att_ref[...], full_ref[:, columns]).astype(BF16)

    for copy in dp_copies:
        copy.wait_recv()
    total = csum[ndp - 1].astype(F32)
    for step in range(ndp - 1):
        total = total + rbuf[step].astype(F32)
    hsum[...] = total.astype(BF16)

    def part_columns(part):
        return pl.ds(part * wide, wide)

    def sum_copy(part):
        return remote(
            hsum.at[:, part_columns(part)], zbuf.at[chip],
            zsend.at[part], zrecv.at[chip], dp, 2 * part + core,
        )

    for part in range(parts):
        @pl.when(chip != part)
        def _():
            sum_copy(part).start()

    chips = n // 2
    my_half = pl.ds(pl.multiple_of(core * half, 16), half)
    for part in range(parts):
        @pl.when(chip == part)
        def _():
            total = hsum[:, part_columns(part)].astype(F32)
            for other in range(chips):
                if other != part:
                    block = zbuf.at[other]
                    remote(block, block, zsend.at[0], zrecv.at[other], dp, 2 * other + core).wait_recv()
                    total = total + zbuf[other].astype(F32)
            block = final.at[my_half, part_columns(part)]
            final[my_half, part_columns(part)] = total.astype(BF16)
            for other in range(chips):
                if other != part:
                    remote(block, block, bsend.at[other], brecv.at[part], dp, 2 * other + core).start()

    def part_block(part):
        return final.at[my_half, part_columns(part)]

    for turn in range(parts):
        part = turn
        block = part_block(part)

        @pl.when(chip != part)
        def _():
            remote(block, block, bsend.at[0], brecv.at[part], dp, 2 * part + core).wait_recv()

        remote(block, block, fsend.at[part], frecv.at[part], dp, sibling).start()
    for part in range(parts):
        theirs = final.at[pl.ds(pl.multiple_of((1 - core) * half, 16), half), part_columns(part)]
        remote(theirs, theirs, fsend.at[part], frecv.at[part], dp, sibling).wait_recv()
    wg_ref[...] = final[...].astype(F32)

    for tensor in range(1, 4):
        receive_home(tensor)
    for slot in range(slots):
        @pl.when(head_in_slot(me, slot, n)[1])
        def _():
            for tensor in range(4):
                for step in range(1, n):
                    home_copy(slot, tensor, step)[1].wait_send()
    for copy in sib_copies + dp_copies:
        copy.wait_send()
    for part in range(parts):
        block = part_block(part)
        remote(block, block, fsend.at[part], frecv.at[part], dp, sibling).wait_send()

        @pl.when(chip != part)
        def _():
            sum_copy(part).wait_send()

        @pl.when(chip == part)
        def _():
            for other in range(chips):
                if other != part:
                    remote(block, block, bsend.at[other], brecv.at[part], dp, 2 * other + core).wait_send()


def segment_ids(length_row, row_total):
    order = lax.iota(jnp.int32, length_row.shape[0])
    segment_ends = jnp.sum(jnp.where(order[None, :] <= order[:, None], length_row[None, :], 0), axis=1)
    positions = lax.iota(jnp.int32, row_total)
    return jnp.sum((segment_ends[None, :] <= positions[:, None]).astype(jnp.int32), axis=1)


def vmem(count):
    return [pl.BlockSpec(memory_space=pltpu.VMEM)] * count


def local(queries, keys, values, seg_lengths, out_grad, w_out):
    n, ndp = lax.axis_size("ctx"), lax.axis_size("dp")
    rows, inner = queries.shape[1:]
    width = out_grad.shape[2]
    seq = rows * n
    wrows = w_out.shape[0]
    half = wrows // 2
    slots = -(-HEADS // n)
    parts = math.gcd(n // 2, width // 128)
    wide = width // parts
    shape = jax.ShapeDtypeStruct
    dma = pltpu.SemaphoreType.DMA
    heads, full = pl.pallas_call(
        functools.partial(scatter_kernel, n, ndp),
        out_shape=(shape((slots, 4, seq, HD), BF16), shape((inner, width), BF16)),
        in_specs=vmem(5),
        out_specs=tuple(vmem(2)),
        scratch_shapes=[
            pltpu.VMEM((rows, inner), BF16),
            dma((4, HEADS)), dma((slots, 4)), dma((ndp,)), dma((ndp,)), dma((ndp,)), dma((ndp,)),
        ],
        compiler_params=pltpu.CompilerParams(
            collective_id=0, has_side_effects=True, vmem_limit_bytes=VMEM_BYTES
        ),
    )(queries[0], keys[0], values[0], out_grad[0], w_out)

    segments = segment_ids(seg_lengths[0], seq)
    results = pl.pallas_call(
        functools.partial(attention_kernel, n, 256),
        out_shape=shape((slots, 4, seq, HD), BF16),
        in_specs=vmem(3),
        out_specs=vmem(1)[0],
        scratch_shapes=[pltpu.VMEM((seq, HD), F32), pltpu.VMEM((seq, HD), F32)],
        compiler_params=pltpu.CompilerParams(vmem_limit_bytes=VMEM_BYTES),
    )(heads, segments[:, None], segments[None, :])

    attended, query_grad, key_grad, value_grad, weight_grad = pl.pallas_call(
        functools.partial(home_kernel, n, ndp, parts),
        out_shape=(
            shape((rows, width), BF16), shape((rows, inner), BF16), shape((rows, inner), BF16),
            shape((rows, inner), BF16), shape((wrows, width), F32),
        ),
        in_specs=vmem(3),
        out_specs=tuple(vmem(5)),
        scratch_shapes=[
            pltpu.VMEM((rows, inner), BF16),
            pltpu.VMEM((inner, rows), BF16),
            pltpu.VMEM((ndp, half, width), BF16),
            pltpu.VMEM((ndp, half, width), BF16),
            pltpu.VMEM((ndp, half, width), BF16),
            pltpu.VMEM((ndp - 1, half, width), BF16),
            pltpu.VMEM((half, width), BF16),
            pltpu.VMEM((n // 2, half, wide), BF16),
            pltpu.VMEM((wrows, width), BF16),
            dma((4, slots, n)), dma((4, HEADS)), dma((ndp,)), dma((ndp,)), dma((ndp,)), dma((ndp,)),
            dma((parts,)), dma((n // 2,)), dma((n // 2,)), dma((parts,)), dma((parts,)), dma((parts,)),
        ],
        compiler_params=pltpu.CompilerParams(
            collective_id=1, has_side_effects=True, vmem_limit_bytes=VMEM_BYTES
        ),
    )(results, full, out_grad[0])
    return (attended[None], query_grad[None], key_grad[None], value_grad[None], weight_grad)


def solution(mesh):
    in_specs = (
        P("dp", "ctx", None),
        P("dp", "ctx", None),
        P("dp", "ctx", None),
        P("dp", None),
        P("dp", "ctx", None),
        P("dp", None),
    )
    out_specs = (
        P("dp", "ctx", None),
        P("dp", "ctx", None),
        P("dp", "ctx", None),
        P("dp", "ctx", None),
        P("dp", None),
    )
    return jax.shard_map(local, mesh=mesh, in_specs=in_specs, out_specs=out_specs, check_vma=False)
```

```python
import functools
import math

import jax
import jax.numpy as jnp
from jax import lax
from jax.experimental import pallas as pl
from jax.experimental.pallas import tpu as pltpu
from jax.sharding import PartitionSpec as P

HEADS = 10
HD = 128
MASKED_SCORE = -1e30
MESH = pl.DeviceIdType.MESH
BF16 = jnp.bfloat16
F32 = jnp.float32
VMEM_BYTES = 56 * 1024 * 1024


def owner_of(head, n):
    slot, place = divmod(head, n)
    if slot and 2 * place + 2 < n:
        place = 2 * place + 2
    return place, slot


def head_in_slot(me, slot, n):
    if slot == 0:
        return me, me < HEADS
    head, valid = 0, False
    for h in range(slot * n, min(HEADS, (slot + 1) * n)):
        place = owner_of(h, n)[0]
        head = jnp.where(me == place, h, head)
        valid = jnp.logical_or(valid, me == place)
    return head, valid


def dot_nt(a, b):
    return lax.dot_general(a, b, (((1,), (1,)), ((), ())), preferred_element_type=F32)


def dot_tn(a, b):
    return lax.dot_general(a, b, (((0,), (0,)), ((), ())), preferred_element_type=F32)


def dot_nn(a, b):
    return jnp.dot(a, b, preferred_element_type=F32)


def remote(src, dst, send, recv, dp, ctx):
    return pltpu.make_async_remote_copy(
        src_ref=src, dst_ref=dst, send_sem=send, recv_sem=recv, device_id=(dp, ctx), device_id_type=MESH
    )


def greet(n, ndp):
    me, dp = lax.axis_index("ctx"), lax.axis_index("dp")
    barrier = pltpu.get_barrier_semaphore()
    for step in range(1, n):
        pl.semaphore_signal(barrier, inc=1, device_id=(dp, lax.rem(me + step, n)), device_id_type=MESH)
    for step in range(1, ndp):
        pl.semaphore_signal(barrier, inc=1, device_id=(lax.rem(dp + step, ndp), me), device_id_type=MESH)
    pl.semaphore_wait(barrier, n - 1 + ndp - 1)


def whole_kernel(
    n, ndp, parts, block,
    q_ref, k_ref, v_ref, og_ref, w_ref, seg_col_ref, seg_row_ref,
    attended_ref, qg_ref, kg_ref, vg_ref, wg_ref,
    heads_ref, full_ref, grad_ref, result_ref, norm_ref, key_sum, value_sum,
    att_ref, att_t, xsend_buf, xrecv_buf, csum, rbuf, hsum, zbuf, final,
    send_sem, recv_sem, wsend, wrecv, gsend, grecv,
    hsend, hrecv, xsend, xrecv, rsend, rrecv, zsend, zrecv, bsend, brecv, fsend, frecv,
):
    me, dp = lax.axis_index("ctx"), lax.axis_index("dp")
    core = lax.rem(me, 2)
    chip = me // 2
    chips = n // 2
    sibling = me + 1 - 2 * core
    slots, _, seq, _ = heads_ref.shape
    rows = q_ref.shape[0]
    width = og_ref.shape[1]
    wrows = w_ref.shape[0]
    half = wrows // 2
    wide = width // parts
    scale = 1.0 / math.sqrt(HD)
    my_rows = pl.ds(pl.multiple_of(me * rows, rows), rows)
    greet(n, ndp)

    def weight_rows(owner, which):
        return pl.ds(pl.multiple_of(owner * wrows + which * half, 16), half)

    weight_copies = []
    for step in range(1, ndp):
        copy = remote(
            w_ref.at[pl.ds(pl.multiple_of(core * half, 16), half)],
            full_ref.at[weight_rows(dp, core)],
            wsend.at[step], wrecv.at[step], lax.rem(dp + step, ndp), me,
        )
        copy.start()
        weight_copies.append(copy)

    def send_head(tensor, source, head, start):
        place, slot = owner_of(head, n)
        columns = pl.ds(head * HD, HD)
        copy = remote(
            source.at[:, columns], heads_ref.at[slot, tensor, my_rows],
            send_sem.at[tensor, head], recv_sem.at[slot, tensor], dp, place,
        )

        @pl.when(me != place)
        def _():
            if start:
                copy.start()
            else:
                copy.wait_send()

        if start:
            @pl.when(me == place)
            def _():
                heads_ref[slot, tensor, my_rows, :] = source[:, columns]

    def await_head(slot, tensor):
        waited = heads_ref.at[slot, tensor, pl.ds(0, rows * (n - 1))]
        pltpu.make_async_copy(waited, waited, recv_sem.at[slot, tensor]).wait()

    targets = (att_ref, qg_ref, kg_ref, vg_ref)

    def home_copy(slot, tensor, step):
        head, _ = head_in_slot(me, slot, n)
        other = lax.rem(me + step, n)
        columns = pl.ds(pl.multiple_of(head * HD, HD), HD)
        source = result_ref.at[slot, tensor, pl.ds(pl.multiple_of(other * rows, rows), rows)]
        return remote(
            source, targets[tensor].at[:, columns],
            hsend.at[tensor, slot, step], hrecv.at[tensor, head], dp, other,
        )

    def send_home(slot, tensor):
        head, _ = head_in_slot(me, slot, n)
        for step in range(1, n):
            home_copy(slot, tensor, step).start()
        columns = pl.ds(pl.multiple_of(head * HD, HD), HD)
        targets[tensor][:, columns] = result_ref[slot, tensor, my_rows, :]

    def receive_home(tensor):
        for head in range(HEADS):
            place, _ = owner_of(head, n)

            @pl.when(me != place)
            def _():
                landed = targets[tensor].at[:, pl.ds(head * HD, HD)]
                remote(landed, landed, hsend.at[tensor, 0, 0], hrecv.at[tensor, head], dp, place).wait_recv()

    for tensor, source in enumerate((q_ref, k_ref, v_ref)):
        for head in range(HEADS):
            send_head(tensor, source, head, True)
    full_ref[pl.ds(pl.multiple_of(dp * wrows, 16), wrows), :] = w_ref[...]

    def block_scores(slot, span):
        seen = seg_col_ref[span, :] == seg_row_ref[...]
        scores = dot_nt(heads_ref[slot, 0, span, :], heads_ref[slot, 1]) * scale
        return jnp.where(seen, scores, MASKED_SCORE)

    for slot in range(slots):
        @pl.when(head_in_slot(me, slot, n)[1])
        def _():
            for tensor in range(3):
                await_head(slot, tensor)

            @pl.loop(0, seq // block)
            def _(index):
                span = pl.ds(pl.multiple_of(index * block, block), block)
                scores = block_scores(slot, span)
                top = jnp.max(scores, axis=1, keepdims=True)
                shifted = jnp.exp(scores - top)
                total = jnp.sum(shifted, axis=1, keepdims=True)
                norm_ref[slot, span, :] = top + jnp.log(total)
                probs_b = (shifted * (1.0 / total)).astype(BF16)
                result_ref[slot, 0, span, :] = dot_nn(probs_b, heads_ref[slot, 2]).astype(BF16)

            send_home(slot, 0)

    passes = []
    for step in range(1, ndp):
        weight_copies[step - 1].wait_recv()
        source = lax.rem(dp - step + ndp, ndp)
        landed = full_ref.at[weight_rows(source, core)]
        copy = remote(landed, landed, gsend.at[step], grecv.at[step], dp, sibling)
        copy.start()
        passes.append(copy)
    for copy in passes:
        copy.wait_recv()
    for head in range(HEADS):
        columns = pl.ds(head * HD, HD)
        grad_ref[:, columns] = dot_nt(og_ref[...], full_ref[columns, :]).astype(BF16)
        send_head(3, grad_ref, head, True)

    receive_home(0)
    att_t[...] = att_ref[...].T

    def share(owner, which):
        return pl.multiple_of(owner * 2 * half + which * half, 16)

    def part_columns(part):
        return pl.ds(part * wide, wide)

    def owner_at(step):
        return lax.rem(dp + step + 1, ndp)

    def pair_copy(part, step):
        columns = part_columns(part)
        return remote(
            xsend_buf.at[step, :, columns], xrecv_buf.at[step, :, columns],
            xsend.at[step, part], xrecv.at[step, part], dp, sibling,
        )

    def dp_copy(part, step):
        columns = part_columns(part)
        return remote(
            csum.at[step, :, columns], rbuf.at[step, :, columns],
            rsend.at[step, part], rrecv.at[step, part], owner_at(step), me,
        )

    for part in range(parts):
        columns = part_columns(part)
        for step in range(ndp):
            left = att_t[pl.ds(share(owner_at(step), 1 - core), half), :]
            xsend_buf[step, :, columns] = dot_nn(left, og_ref[:, columns]).astype(BF16)
            pair_copy(part, step).start()
    for part in range(parts):
        columns = part_columns(part)
        for step in range(ndp):
            left = att_t[pl.ds(share(owner_at(step), core), half), :]
            mine = dot_nn(left, og_ref[:, columns])
            pair_copy(part, step).wait_recv()
            csum[step, :, columns] = (mine + xrecv_buf[step, :, columns].astype(F32)).astype(BF16)
            if step < ndp - 1:
                dp_copy(part, step).start()

    for slot in range(slots):
        @pl.when(head_in_slot(me, slot, n)[1])
        def _():
            await_head(slot, 3)
            key_sum[...] = jnp.zeros_like(key_sum)
            value_sum[...] = jnp.zeros_like(value_sum)

            @pl.loop(0, seq // block)
            def _(index):
                span = pl.ds(pl.multiple_of(index * block, block), block)
                grad = heads_ref[slot, 3, span, :]
                probs = jnp.exp(block_scores(slot, span) - norm_ref[slot, span, :])
                attention = result_ref[slot, 0, span, :]
                grad_dot = jnp.sum(grad.astype(F32) * attention.astype(F32), axis=1, keepdims=True)
                dscore = (probs * (dot_nt(grad, heads_ref[slot, 2]) - grad_dot)).astype(BF16)
                result_ref[slot, 1, span, :] = (dot_nn(dscore, heads_ref[slot, 1]) * scale).astype(BF16)
                key_sum[...] += dot_tn(dscore, heads_ref[slot, 0, span, :])
                value_sum[...] += dot_tn(probs.astype(BF16), grad)

            result_ref[slot, 2] = (key_sum[...] * scale).astype(BF16)
            result_ref[slot, 3] = value_sum[...].astype(BF16)
            for tensor in range(1, 4):
                send_home(slot, tensor)

    @pl.loop(0, width // 512)
    def _(index):
        columns = pl.ds(pl.multiple_of(index * 512, 512), 512)
        attended_ref[:, columns] = dot_nn(att_ref[...], full_ref[:, columns]).astype(BF16)

    my_half = pl.ds(pl.multiple_of(core * half, 16), half)
    their_half = pl.ds(pl.multiple_of((1 - core) * half, 16), half)

    def sum_copy(part):
        return remote(
            hsum.at[:, part_columns(part)], zbuf.at[chip],
            zsend.at[part], zrecv.at[chip], dp, 2 * part + core,
        )

    def spread_copy(part, other):
        landed = final.at[my_half, part_columns(part)]
        return remote(landed, landed, bsend.at[other], brecv.at[part], dp, 2 * other + core)

    def pass_copy(part, span):
        landed = final.at[span, part_columns(part)]
        return remote(landed, landed, fsend.at[part], frecv.at[part], dp, sibling)

    def finish(part):
        @pl.when(chip == part)
        def _():
            total = hsum[:, part_columns(part)].astype(F32)
            for other in range(chips):
                if other != part:
                    landed = zbuf.at[other]
                    remote(landed, landed, zsend.at[0], zrecv.at[other], dp, 2 * other + core).wait_recv()
                    total = total + zbuf[other].astype(F32)
            final[my_half, part_columns(part)] = total.astype(BF16)
            for other in range(chips):
                if other != part:
                    spread_copy(part, other).start()

    for part in range(parts):
        columns = part_columns(part)
        total = csum[ndp - 1, :, columns].astype(F32)
        for step in range(ndp - 1):
            dp_copy(part, step).wait_recv()
            total = total + rbuf[step, :, columns].astype(F32)
        hsum[:, columns] = total.astype(BF16)

        @pl.when(chip != part)
        def _():
            sum_copy(part).start()

        if part:
            finish(part - 1)
    finish(parts - 1)

    for part in range(parts):
        @pl.when(chip != part)
        def _():
            spread_copy(part, part).wait_recv()

        pass_copy(part, my_half).start()
    for part in range(parts):
        pass_copy(part, their_half).wait_recv()
    wg_ref[...] = final[...].astype(F32)

    for tensor in range(1, 4):
        receive_home(tensor)
    for tensor, source in enumerate((q_ref, k_ref, v_ref, grad_ref)):
        for head in range(HEADS):
            send_head(tensor, source, head, False)
    for copy in weight_copies + passes:
        copy.wait_send()
    for slot in range(slots):
        @pl.when(head_in_slot(me, slot, n)[1])
        def _():
            for tensor in range(4):
                for step in range(1, n):
                    home_copy(slot, tensor, step).wait_send()
    for part in range(parts):
        for step in range(ndp):
            pair_copy(part, step).wait_send()
            if step < ndp - 1:
                dp_copy(part, step).wait_send()
        pass_copy(part, my_half).wait_send()

        @pl.when(chip != part)
        def _():
            sum_copy(part).wait_send()

        @pl.when(chip == part)
        def _():
            for other in range(chips):
                if other != part:
                    spread_copy(part, other).wait_send()


def copy_kernel(*refs):
    count = len(refs) // 2
    sems = refs[-1]
    copies = [pltpu.make_async_copy(refs[i], refs[count + i], sems.at[i]) for i in range(count)]
    for copy in copies:
        copy.start()
    for copy in copies:
        copy.wait()


def segment_ids(length_row, row_total):
    order = lax.iota(jnp.int32, length_row.shape[0])
    segment_ends = jnp.sum(jnp.where(order[None, :] <= order[:, None], length_row[None, :], 0), axis=1)
    positions = lax.iota(jnp.int32, row_total)
    return jnp.sum((segment_ends[None, :] <= positions[:, None]).astype(jnp.int32), axis=1)


def vmem(count):
    return [pl.BlockSpec(memory_space=pltpu.VMEM)] * count


def local(queries, keys, values, seg_lengths, out_grad, w_out):
    n, ndp = lax.axis_size("ctx"), lax.axis_size("dp")
    rows, inner = queries.shape[1:]
    width = out_grad.shape[2]
    seq = rows * n
    wrows = w_out.shape[0]
    half = wrows // 2
    slots = -(-HEADS // n)
    parts = math.gcd(n // 2, width // 128)
    wide = width // parts
    shape = jax.ShapeDtypeStruct
    dma = pltpu.SemaphoreType.DMA
    segments = segment_ids(seg_lengths[0], seq)
    out_shape = (
        shape((rows, width), BF16), shape((rows, inner), BF16), shape((rows, inner), BF16),
        shape((rows, inner), BF16), shape((wrows, width), F32),
    )
    outputs = pl.pallas_call(
        functools.partial(whole_kernel, n, ndp, parts, 256),
        out_shape=out_shape,
        in_specs=vmem(7),
        out_specs=tuple(vmem(5)),
        scratch_shapes=[
            pltpu.VMEM((slots, 4, seq, HD), BF16),
            pltpu.VMEM((inner, width), BF16),
            pltpu.VMEM((rows, inner), BF16),
            pltpu.VMEM((slots, 4, seq, HD), BF16),
            pltpu.VMEM((slots, seq, 1), F32),
            pltpu.VMEM((seq, HD), F32),
            pltpu.VMEM((seq, HD), F32),
            pltpu.VMEM((rows, inner), BF16),
            pltpu.VMEM((inner, rows), BF16),
            pltpu.VMEM((ndp, half, width), BF16),
            pltpu.VMEM((ndp, half, width), BF16),
            pltpu.VMEM((ndp, half, width), BF16),
            pltpu.VMEM((ndp - 1, half, width), BF16),
            pltpu.VMEM((half, width), BF16),
            pltpu.VMEM((n // 2, half, wide), BF16),
            pltpu.VMEM((wrows, width), BF16),
            dma((4, HEADS)), dma((slots, 4)), dma((ndp,)), dma((ndp,)), dma((ndp,)), dma((ndp,)),
            dma((4, slots, n)), dma((4, HEADS)),
            dma((ndp, parts)), dma((ndp, parts)), dma((ndp, parts)), dma((ndp, parts)),
            dma((parts,)), dma((n // 2,)), dma((n // 2,)), dma((parts,)), dma((parts,)), dma((parts,)),
        ],
        compiler_params=pltpu.CompilerParams(
            collective_id=0, has_side_effects=True, vmem_limit_bytes=VMEM_BYTES
        ),
    )(queries[0], keys[0], values[0], out_grad[0], w_out, segments[:, None], segments[None, :])
    anywhere = [pl.BlockSpec(memory_space=pl.ANY)] * 5
    attended, query_grad, key_grad, value_grad, weight_grad = pl.pallas_call(
        copy_kernel,
        out_shape=out_shape,
        in_specs=anywhere,
        out_specs=tuple(anywhere),
        scratch_shapes=[dma((5,))],
    )(*outputs)
    return (attended[None], query_grad[None], key_grad[None], value_grad[None], weight_grad)


def solution(mesh):
    in_specs = (
        P("dp", "ctx", None),
        P("dp", "ctx", None),
        P("dp", "ctx", None),
        P("dp", None),
        P("dp", "ctx", None),
        P("dp", None),
    )
    out_specs = (
        P("dp", "ctx", None),
        P("dp", "ctx", None),
        P("dp", "ctx", None),
        P("dp", "ctx", None),
        P("dp", None),
    )
    return jax.shard_map(local, mesh=mesh, in_specs=in_specs, out_specs=out_specs, check_vma=False)
```

```python
import functools
import math

import jax
import jax.numpy as jnp
from jax import lax
from jax.experimental import pallas as pl
from jax.experimental.pallas import tpu as pltpu
from jax.sharding import PartitionSpec as P

HEADS = 10
HD = 128
MASKED_SCORE = -1e30
MESH = pl.DeviceIdType.MESH
BF16 = jnp.bfloat16
F32 = jnp.float32
VMEM_BYTES = 56 * 1024 * 1024


def owner_of(head, n):
    slot, place = divmod(head, n)
    if slot and 2 * place + 2 < n:
        place = 2 * place + 2
    return place, slot


def head_in_slot(me, slot, n):
    if slot == 0:
        return me, me < HEADS
    head, valid = 0, False
    for h in range(slot * n, min(HEADS, (slot + 1) * n)):
        place = owner_of(h, n)[0]
        head = jnp.where(me == place, h, head)
        valid = jnp.logical_or(valid, me == place)
    return head, valid


def dot_nt(a, b):
    return lax.dot_general(a, b, (((1,), (1,)), ((), ())), preferred_element_type=F32)


def dot_tn(a, b):
    return lax.dot_general(a, b, (((0,), (0,)), ((), ())), preferred_element_type=F32)


def dot_nn(a, b):
    return jnp.dot(a, b, preferred_element_type=F32)


def remote(src, dst, send, recv, dp, ctx):
    return pltpu.make_async_remote_copy(
        src_ref=src, dst_ref=dst, send_sem=send, recv_sem=recv, device_id=(dp, ctx), device_id_type=MESH
    )


def greet(n, ndp):
    me, dp = lax.axis_index("ctx"), lax.axis_index("dp")
    barrier = pltpu.get_barrier_semaphore()
    for step in range(1, n):
        pl.semaphore_signal(barrier, inc=1, device_id=(dp, lax.rem(me + step, n)), device_id_type=MESH)
    for step in range(1, ndp):
        pl.semaphore_signal(barrier, inc=1, device_id=(lax.rem(dp + step, ndp), me), device_id_type=MESH)
    pl.semaphore_wait(barrier, n - 1 + ndp - 1)


def whole_kernel(
    n, ndp, parts, block,
    q_ref, k_ref, v_ref, og_ref, w_ref, seg_col_ref, seg_row_ref,
    attended_ref, qg_ref, kg_ref, vg_ref, wg_ref,
    heads_ref, full_ref, grad_ref, result_ref, norm_ref, key_sum, value_sum,
    att_ref, att_t, xsend_buf, xrecv_buf, csum, rbuf, hsum, zbuf, acc, final,
    send_sem, recv_sem, wsend, wrecv, gsend, grecv,
    hsend, hrecv, xsend, xrecv, rsend, rrecv, zsend, zrecv, bsend, brecv, fsend, frecv,
):
    me, dp = lax.axis_index("ctx"), lax.axis_index("dp")
    core = lax.rem(me, 2)
    chip = me // 2
    chips = n // 2
    sibling = me + 1 - 2 * core
    slots, _, seq, _ = heads_ref.shape
    rows = q_ref.shape[0]
    width = og_ref.shape[1]
    wrows = w_ref.shape[0]
    half = wrows // 2
    wide = width // parts
    scale = 1.0 / math.sqrt(HD)
    my_rows = pl.ds(pl.multiple_of(me * rows, rows), rows)
    greet(n, ndp)

    def weight_rows(owner, which):
        return pl.ds(pl.multiple_of(owner * wrows + which * half, 16), half)

    weight_copies = []
    for step in range(1, ndp):
        copy = remote(
            w_ref.at[pl.ds(pl.multiple_of(core * half, 16), half)],
            full_ref.at[weight_rows(dp, core)],
            wsend.at[step], wrecv.at[step], lax.rem(dp + step, ndp), me,
        )
        copy.start()
        weight_copies.append(copy)

    def send_head(tensor, source, head, start):
        place, slot = owner_of(head, n)
        columns = pl.ds(head * HD, HD)
        copy = remote(
            source.at[:, columns], heads_ref.at[slot, tensor, my_rows],
            send_sem.at[tensor, head], recv_sem.at[slot, tensor], dp, place,
        )

        @pl.when(me != place)
        def _():
            if start:
                copy.start()
            else:
                copy.wait_send()

        if start:
            @pl.when(me == place)
            def _():
                heads_ref[slot, tensor, my_rows, :] = source[:, columns]

    def await_head(slot, tensor):
        waited = heads_ref.at[slot, tensor, pl.ds(0, rows * (n - 1))]
        pltpu.make_async_copy(waited, waited, recv_sem.at[slot, tensor]).wait()

    targets = (att_ref, qg_ref, kg_ref, vg_ref)

    def home_copy(slot, tensor, step):
        head, _ = head_in_slot(me, slot, n)
        other = lax.rem(me + step, n)
        columns = pl.ds(pl.multiple_of(head * HD, HD), HD)
        source = result_ref.at[slot, tensor, pl.ds(pl.multiple_of(other * rows, rows), rows)]
        return remote(
            source, targets[tensor].at[:, columns],
            hsend.at[tensor, slot, step], hrecv.at[tensor, head], dp, other,
        )

    def send_home(slot, tensor):
        head, _ = head_in_slot(me, slot, n)
        for step in range(1, n):
            home_copy(slot, tensor, step).start()
        columns = pl.ds(pl.multiple_of(head * HD, HD), HD)
        targets[tensor][:, columns] = result_ref[slot, tensor, my_rows, :]

    def receive_home(tensor):
        for head in range(HEADS):
            place, _ = owner_of(head, n)

            @pl.when(me != place)
            def _():
                landed = targets[tensor].at[:, pl.ds(head * HD, HD)]
                remote(landed, landed, hsend.at[tensor, 0, 0], hrecv.at[tensor, head], dp, place).wait_recv()

    for tensor, source in enumerate((q_ref, k_ref, v_ref)):
        for head in range(HEADS):
            send_head(tensor, source, head, True)
    full_ref[pl.ds(pl.multiple_of(dp * wrows, 16), wrows), :] = w_ref[...]

    def block_scores(slot, span):
        seen = seg_col_ref[span, :] == seg_row_ref[...]
        scores = dot_nt(heads_ref[slot, 0, span, :], heads_ref[slot, 1]) * scale
        return jnp.where(seen, scores, MASKED_SCORE)

    for slot in range(slots):
        @pl.when(head_in_slot(me, slot, n)[1])
        def _():
            for tensor in range(3):
                await_head(slot, tensor)

            @pl.loop(0, seq // block)
            def _(index):
                span = pl.ds(pl.multiple_of(index * block, block), block)
                scores = block_scores(slot, span)
                top = jnp.max(scores, axis=1, keepdims=True)
                shifted = jnp.exp(scores - top)
                total = jnp.sum(shifted, axis=1, keepdims=True)
                norm_ref[slot, span, :] = top + jnp.log(total)
                probs_b = (shifted * (1.0 / total)).astype(BF16)
                result_ref[slot, 0, span, :] = dot_nn(probs_b, heads_ref[slot, 2]).astype(BF16)

            send_home(slot, 0)

    receive_home(0)
    att_t[...] = att_ref[...].T

    def share(owner, which):
        return pl.multiple_of(owner * 2 * half + which * half, 16)

    def part_columns(part):
        return pl.ds(part * wide, wide)

    def owner_at(step):
        return lax.rem(dp + step + 1, ndp)

    def pair_copy(part, step):
        columns = part_columns(part)
        return remote(
            xsend_buf.at[step, :, columns], xrecv_buf.at[step, :, columns],
            xsend.at[step, part], xrecv.at[step, part], dp, sibling,
        )

    def dp_copy(part, step):
        columns = part_columns(part)
        return remote(
            csum.at[step, :, columns], rbuf.at[step, :, columns],
            rsend.at[step, part], rrecv.at[step, part], owner_at(step), me,
        )

    for part in range(parts):
        columns = part_columns(part)
        for step in range(ndp):
            left = att_t[pl.ds(share(owner_at(step), 1 - core), half), :]
            xsend_buf[step, :, columns] = dot_nn(left, og_ref[:, columns]).astype(BF16)
            pair_copy(part, step).start()
    passes = []
    for step in range(1, ndp):
        weight_copies[step - 1].wait_recv()
        source = lax.rem(dp - step + ndp, ndp)
        landed = full_ref.at[weight_rows(source, core)]
        copy = remote(landed, landed, gsend.at[step], grecv.at[step], dp, sibling)
        copy.start()
        passes.append(copy)
    for copy in passes:
        copy.wait_recv()
    for head in range(HEADS):
        columns = pl.ds(head * HD, HD)
        grad_ref[:, columns] = dot_nt(og_ref[...], full_ref[columns, :]).astype(BF16)
        send_head(3, grad_ref, head, True)

    for part in range(parts):
        columns = part_columns(part)
        for step in range(ndp):
            left = att_t[pl.ds(share(owner_at(step), core), half), :]
            mine = dot_nn(left, og_ref[:, columns])
            pair_copy(part, step).wait_recv()
            csum[step, :, columns] = (mine + xrecv_buf[step, :, columns].astype(F32)).astype(BF16)
            if step < ndp - 1:
                dp_copy(part, step).start()

    for slot in range(slots):
        @pl.when(head_in_slot(me, slot, n)[1])
        def _():
            await_head(slot, 3)
            key_sum[...] = jnp.zeros_like(key_sum)
            value_sum[...] = jnp.zeros_like(value_sum)

            @pl.loop(0, seq // block)
            def _(index):
                span = pl.ds(pl.multiple_of(index * block, block), block)
                grad = heads_ref[slot, 3, span, :]
                probs = jnp.exp(block_scores(slot, span) - norm_ref[slot, span, :])
                attention = result_ref[slot, 0, span, :]
                grad_dot = jnp.sum(grad.astype(F32) * attention.astype(F32), axis=1, keepdims=True)
                dscore = (probs * (dot_nt(grad, heads_ref[slot, 2]) - grad_dot)).astype(BF16)
                result_ref[slot, 1, span, :] = (dot_nn(dscore, heads_ref[slot, 1]) * scale).astype(BF16)
                key_sum[...] += dot_tn(dscore, heads_ref[slot, 0, span, :])
                value_sum[...] += dot_tn(probs.astype(BF16), grad)

            result_ref[slot, 2] = (key_sum[...] * scale).astype(BF16)
            result_ref[slot, 3] = value_sum[...].astype(BF16)
            for tensor in range(1, 4):
                send_home(slot, tensor)

    @pl.loop(0, width // 512)
    def _(index):
        columns = pl.ds(pl.multiple_of(index * 512, 512), 512)
        attended_ref[:, columns] = dot_nn(att_ref[...], full_ref[:, columns]).astype(BF16)

    my_half = pl.ds(pl.multiple_of(core * half, 16), half)
    their_half = pl.ds(pl.multiple_of((1 - core) * half, 16), half)

    right, left_side = lax.rem(me + 2, n), lax.rem(me + n - 2, n)

    def goes_left(part):
        return jnp.logical_and(chip > 0, chip <= part)

    def goes_right(part):
        return jnp.logical_and(chip < chips - 1, chip >= part)

    def sum_copy(part, side):
        return remote(
            hsum.at[:, part_columns(part)], zbuf.at[side, part],
            zsend.at[part], zrecv.at[side, part], dp, right if side == 0 else left_side,
        )

    def spread_copy(part, side):
        landed = final.at[my_half, part_columns(part)]
        return remote(
            landed, landed, bsend.at[part, side], brecv.at[part], dp, left_side if side == 0 else right
        )

    def pass_copy(part, span):
        landed = final.at[span, part_columns(part)]
        return remote(landed, landed, fsend.at[part], frecv.at[part], dp, sibling)

    def reduce_part(part):
        columns = part_columns(part)
        total = csum[ndp - 1, :, columns].astype(F32)
        for step in range(ndp - 1):
            dp_copy(part, step).wait_recv()
            total = total + rbuf[step, :, columns].astype(F32)
        acc[...] = total
        for side, comes in ((0, goes_left(part)), (1, goes_right(part))):
            @pl.when(comes)
            def _():
                sum_copy(part, side).wait_recv()
                acc[...] += zbuf[side, part].astype(F32)

        for side, onward in ((0, chip < part), (1, chip > part)):
            @pl.when(onward)
            def _():
                hsum[:, columns] = acc[...].astype(BF16)
                sum_copy(part, side).start()

        @pl.when(chip == part)
        def _():
            final[my_half, columns] = acc[...].astype(BF16)

    def spread_part(part):
        @pl.when(chip != part)
        def _():
            spread_copy(part, 0).wait_recv()

        for side, onward in ((0, goes_left(part)), (1, goes_right(part))):
            @pl.when(onward)
            def _():
                spread_copy(part, side).start()

        pass_copy(part, my_half).start()

    order = (0, 3, 1, 2) if parts == 4 else tuple(range(parts))
    for turn, part in enumerate(order):
        reduce_part(part)
        if turn > 1:
            spread_part(order[turn - 2])
    for part in order[max(0, parts - 2):]:
        spread_part(part)
    for part in range(parts):
        pass_copy(part, their_half).wait_recv()
    wg_ref[...] = final[...]

    for tensor in range(1, 4):
        receive_home(tensor)
    for tensor, source in enumerate((q_ref, k_ref, v_ref, grad_ref)):
        for head in range(HEADS):
            send_head(tensor, source, head, False)
    for copy in weight_copies + passes:
        copy.wait_send()
    for slot in range(slots):
        @pl.when(head_in_slot(me, slot, n)[1])
        def _():
            for tensor in range(4):
                for step in range(1, n):
                    home_copy(slot, tensor, step).wait_send()
    for part in range(parts):
        for step in range(ndp):
            pair_copy(part, step).wait_send()
            if step < ndp - 1:
                dp_copy(part, step).wait_send()
        pass_copy(part, my_half).wait_send()

        @pl.when(chip != part)
        def _():
            sum_copy(part, 0).wait_send()

        for side, onward in ((0, goes_left(part)), (1, goes_right(part))):
            @pl.when(onward)
            def _():
                spread_copy(part, side).wait_send()


def copy_kernel(*refs):
    sources, targets, held = refs[:5], refs[5:10], refs[10:15]
    wide_held, in_sem, out_sem = refs[15:]
    loads = [pltpu.make_async_copy(sources[i], held[i], in_sem.at[i]) for i in range(5)]
    stores = [
        pltpu.make_async_copy(held[i] if i < 4 else wide_held, targets[i], out_sem.at[i]) for i in range(5)
    ]
    for i in (4, 0, 1, 2, 3):
        loads[i].start()
    loads[4].wait()
    wide_held[...] = held[4][...].astype(F32)
    stores[4].start()
    for i in range(4):
        loads[i].wait()
        stores[i].start()
    for store in stores:
        store.wait()


def segment_ids(length_row, row_total):
    order = lax.iota(jnp.int32, length_row.shape[0])
    segment_ends = jnp.sum(jnp.where(order[None, :] <= order[:, None], length_row[None, :], 0), axis=1)
    positions = lax.iota(jnp.int32, row_total)
    return jnp.sum((segment_ends[None, :] <= positions[:, None]).astype(jnp.int32), axis=1)


def vmem(count):
    return [pl.BlockSpec(memory_space=pltpu.VMEM)] * count


def local(queries, keys, values, seg_lengths, out_grad, w_out):
    n, ndp = lax.axis_size("ctx"), lax.axis_size("dp")
    rows, inner = queries.shape[1:]
    width = out_grad.shape[2]
    seq = rows * n
    wrows = w_out.shape[0]
    half = wrows // 2
    slots = -(-HEADS // n)
    parts = math.gcd(n // 2, width // 128)
    wide = width // parts
    shape = jax.ShapeDtypeStruct
    dma = pltpu.SemaphoreType.DMA
    segments = segment_ids(seg_lengths[0], seq)
    out_shape = (
        shape((rows, width), BF16), shape((rows, inner), BF16), shape((rows, inner), BF16),
        shape((rows, inner), BF16), shape((wrows, width), F32),
    )
    outputs = pl.pallas_call(
        functools.partial(whole_kernel, n, ndp, parts, 256),
        out_shape=out_shape[:4] + (shape((wrows, width), BF16),),
        in_specs=vmem(7),
        out_specs=tuple(vmem(5)),
        scratch_shapes=[
            pltpu.VMEM((slots, 4, seq, HD), BF16),
            pltpu.VMEM((inner, width), BF16),
            pltpu.VMEM((rows, inner), BF16),
            pltpu.VMEM((slots, 4, seq, HD), BF16),
            pltpu.VMEM((slots, seq, 1), F32),
            pltpu.VMEM((seq, HD), F32),
            pltpu.VMEM((seq, HD), F32),
            pltpu.VMEM((rows, inner), BF16),
            pltpu.VMEM((inner, rows), BF16),
            pltpu.VMEM((ndp, half, width), BF16),
            pltpu.VMEM((ndp, half, width), BF16),
            pltpu.VMEM((ndp, half, width), BF16),
            pltpu.VMEM((ndp - 1, half, width), BF16),
            pltpu.VMEM((half, width), BF16),
            pltpu.VMEM((2, parts, half, wide), BF16),
            pltpu.VMEM((half, wide), F32),
            pltpu.VMEM((wrows, width), BF16),
            dma((4, HEADS)), dma((slots, 4)), dma((ndp,)), dma((ndp,)), dma((ndp,)), dma((ndp,)),
            dma((4, slots, n)), dma((4, HEADS)),
            dma((ndp, parts)), dma((ndp, parts)), dma((ndp, parts)), dma((ndp, parts)),
            dma((parts,)), dma((2, parts)), dma((parts, 2)), dma((parts,)), dma((parts,)), dma((parts,)),
        ],
        compiler_params=pltpu.CompilerParams(
            collective_id=0, has_side_effects=True, vmem_limit_bytes=VMEM_BYTES
        ),
    )(queries[0], keys[0], values[0], out_grad[0], w_out, segments[:, None], segments[None, :])
    anywhere = [pl.BlockSpec(memory_space=pl.ANY)] * 5
    attended, query_grad, key_grad, value_grad, weight_grad = pl.pallas_call(
        copy_kernel,
        out_shape=out_shape,
        in_specs=anywhere,
        out_specs=tuple(anywhere),
        scratch_shapes=[pltpu.VMEM(x.shape, BF16) for x in out_shape]
        + [pltpu.VMEM((wrows, width), F32), dma((5,)), dma((5,))],
        compiler_params=pltpu.CompilerParams(vmem_limit_bytes=VMEM_BYTES),
    )(*outputs)
    return (attended[None], query_grad[None], key_grad[None], value_grad[None], weight_grad)


def solution(mesh):
    in_specs = (
        P("dp", "ctx", None),
        P("dp", "ctx", None),
        P("dp", "ctx", None),
        P("dp", None),
        P("dp", "ctx", None),
        P("dp", None),
    )
    out_specs = (
        P("dp", "ctx", None),
        P("dp", "ctx", None),
        P("dp", "ctx", None),
        P("dp", "ctx", None),
        P("dp", None),
    )
    return jax.shard_map(local, mesh=mesh, in_specs=in_specs, out_specs=out_specs, check_vma=False)
```

```python
import functools
import math

import jax
import jax.numpy as jnp
from jax import lax
from jax.experimental import pallas as pl
from jax.experimental.pallas import tpu as pltpu
from jax.sharding import PartitionSpec as P

HEADS = 10
HD = 128
MASKED_SCORE = -1e30
MESH = pl.DeviceIdType.MESH
BF16 = jnp.bfloat16
F32 = jnp.float32
VMEM_BYTES = 56 * 1024 * 1024


def owner_of(head, n):
    slot, place = divmod(head, n)
    if slot and 2 * place + 2 < n:
        place = 2 * place + 2
    return place, slot


def head_in_slot(me, slot, n):
    if slot == 0:
        return me, me < HEADS
    head, valid = 0, False
    for h in range(slot * n, min(HEADS, (slot + 1) * n)):
        place = owner_of(h, n)[0]
        head = jnp.where(me == place, h, head)
        valid = jnp.logical_or(valid, me == place)
    return head, valid


def dot_nt(a, b):
    return lax.dot_general(a, b, (((1,), (1,)), ((), ())), preferred_element_type=F32)


def dot_tn(a, b):
    return lax.dot_general(a, b, (((0,), (0,)), ((), ())), preferred_element_type=F32)


def dot_nn(a, b):
    return jnp.dot(a, b, preferred_element_type=F32)


def remote(src, dst, send, recv, dp, ctx):
    return pltpu.make_async_remote_copy(
        src_ref=src, dst_ref=dst, send_sem=send, recv_sem=recv, device_id=(dp, ctx), device_id_type=MESH
    )


def greet(n, ndp):
    me, dp = lax.axis_index("ctx"), lax.axis_index("dp")
    barrier = pltpu.get_barrier_semaphore()
    for step in range(1, n):
        pl.semaphore_signal(barrier, inc=1, device_id=(dp, lax.rem(me + step, n)), device_id_type=MESH)
    for step in range(1, ndp):
        pl.semaphore_signal(barrier, inc=1, device_id=(lax.rem(dp + step, ndp), me), device_id_type=MESH)
    pl.semaphore_wait(barrier, n - 1 + ndp - 1)


def whole_kernel(
    n, ndp, parts, block,
    q_ref, k_ref, v_ref, og_ref, w_ref, seg_col_ref, seg_row_ref,
    attended_ref, qg_ref, kg_ref, vg_ref, wg_ref,
    heads_ref, full_ref, grad_ref, result_ref, norm_ref, key_sum, value_sum,
    att_ref, att_t, xsend_buf, xrecv_buf, csum, rbuf, hsum, zbuf, final,
    send_sem, recv_sem, wsend, wrecv, gsend, grecv,
    hsend, hrecv, xsend, xrecv, rsend, rrecv, zsend, zrecv, bsend, brecv, fsend, frecv,
):
    me, dp = lax.axis_index("ctx"), lax.axis_index("dp")
    core = lax.rem(me, 2)
    chip = me // 2
    chips = n // 2
    sibling = me + 1 - 2 * core
    slots, _, seq, _ = heads_ref.shape
    rows = q_ref.shape[0]
    width = og_ref.shape[1]
    wrows = w_ref.shape[0]
    half = wrows // 2
    wide = width // parts
    scale = 1.0 / math.sqrt(HD)
    my_rows = pl.ds(pl.multiple_of(me * rows, rows), rows)
    greet(n, ndp)

    def weight_rows(owner, which):
        return pl.ds(pl.multiple_of(owner * wrows + which * half, 16), half)

    weight_copies = []
    for step in range(1, ndp):
        copy = remote(
            w_ref.at[pl.ds(pl.multiple_of(core * half, 16), half)],
            full_ref.at[weight_rows(dp, core)],
            wsend.at[step], wrecv.at[step], lax.rem(dp + step, ndp), me,
        )
        copy.start()
        weight_copies.append(copy)

    def send_head(tensor, source, head, start):
        place, slot = owner_of(head, n)
        columns = pl.ds(head * HD, HD)
        copy = remote(
            source.at[:, columns], heads_ref.at[slot, tensor, my_rows],
            send_sem.at[tensor, head], recv_sem.at[slot, tensor], dp, place,
        )

        @pl.when(me != place)
        def _():
            if start:
                copy.start()
            else:
                copy.wait_send()

        if start:
            @pl.when(me == place)
            def _():
                heads_ref[slot, tensor, my_rows, :] = source[:, columns]

    def await_head(slot, tensor):
        waited = heads_ref.at[slot, tensor, pl.ds(0, rows * (n - 1))]
        pltpu.make_async_copy(waited, waited, recv_sem.at[slot, tensor]).wait()

    targets = (att_ref, qg_ref, kg_ref, vg_ref)

    def home_copy(slot, tensor, step):
        head, _ = head_in_slot(me, slot, n)
        other = lax.rem(me + step, n)
        columns = pl.ds(pl.multiple_of(head * HD, HD), HD)
        source = result_ref.at[slot, tensor, pl.ds(pl.multiple_of(other * rows, rows), rows)]
        return remote(
            source, targets[tensor].at[:, columns],
            hsend.at[tensor, slot, step], hrecv.at[tensor, head], dp, other,
        )

    def send_home(slot, tensor):
        head, _ = head_in_slot(me, slot, n)
        for step in range(1, n):
            home_copy(slot, tensor, step).start()
        columns = pl.ds(pl.multiple_of(head * HD, HD), HD)
        targets[tensor][:, columns] = result_ref[slot, tensor, my_rows, :]

    def receive_home(tensor):
        for head in range(HEADS):
            place, _ = owner_of(head, n)

            @pl.when(me != place)
            def _():
                landed = targets[tensor].at[:, pl.ds(head * HD, HD)]
                remote(landed, landed, hsend.at[tensor, 0, 0], hrecv.at[tensor, head], dp, place).wait_recv()

    for tensor, source in enumerate((q_ref, k_ref, v_ref)):
        for head in range(HEADS):
            send_head(tensor, source, head, True)
    full_ref[pl.ds(pl.multiple_of(dp * wrows, 16), wrows), :] = w_ref[...]

    def block_scores(slot, span):
        seen = seg_col_ref[span, :] == seg_row_ref[...]
        scores = dot_nt(heads_ref[slot, 0, span, :], heads_ref[slot, 1]) * scale
        return jnp.where(seen, scores, MASKED_SCORE)

    for slot in range(slots):
        @pl.when(head_in_slot(me, slot, n)[1])
        def _():
            for tensor in range(3):
                await_head(slot, tensor)

            @pl.loop(0, seq // block)
            def _(index):
                span = pl.ds(pl.multiple_of(index * block, block), block)
                scores = block_scores(slot, span)
                top = jnp.max(scores, axis=1, keepdims=True)
                shifted = jnp.exp(scores - top)
                total = jnp.sum(shifted, axis=1, keepdims=True)
                norm_ref[slot, span, :] = top + jnp.log(total)
                probs_b = (shifted * (1.0 / total)).astype(BF16)
                result_ref[slot, 0, span, :] = dot_nn(probs_b, heads_ref[slot, 2]).astype(BF16)

            send_home(slot, 0)

    passes = []
    for step in range(1, ndp):
        weight_copies[step - 1].wait_recv()
        source = lax.rem(dp - step + ndp, ndp)
        landed = full_ref.at[weight_rows(source, core)]
        copy = remote(landed, landed, gsend.at[step], grecv.at[step], dp, sibling)
        copy.start()
        passes.append(copy)
    for copy in passes:
        copy.wait_recv()
    for head in range(HEADS):
        columns = pl.ds(head * HD, HD)
        grad_ref[:, columns] = dot_nt(og_ref[...], full_ref[columns, :]).astype(BF16)
        send_head(3, grad_ref, head, True)

    receive_home(0)
    att_t[...] = att_ref[...].T

    def share(owner, which):
        return pl.multiple_of(owner * 2 * half + which * half, 16)

    def part_columns(part):
        return pl.ds(part * wide, wide)

    def owner_at(step):
        return lax.rem(dp + step + 1, ndp)

    def pair_copy(part, step):
        columns = part_columns(part)
        return remote(
            xsend_buf.at[step, :, columns], xrecv_buf.at[step, :, columns],
            xsend.at[step, part], xrecv.at[step, part], dp, sibling,
        )

    def dp_copy(part, step):
        columns = part_columns(part)
        return remote(
            csum.at[step, :, columns], rbuf.at[step, :, columns],
            rsend.at[step, part], rrecv.at[step, part], owner_at(step), me,
        )

    for part in range(parts):
        columns = part_columns(part)
        for step in range(ndp):
            left = att_t[pl.ds(share(owner_at(step), 1 - core), half), :]
            xsend_buf[step, :, columns] = dot_nn(left, og_ref[:, columns]).astype(BF16)
            pair_copy(part, step).start()
    for part in range(parts):
        columns = part_columns(part)
        for step in range(ndp):
            left = att_t[pl.ds(share(owner_at(step), core), half), :]
            mine = dot_nn(left, og_ref[:, columns])
            pair_copy(part, step).wait_recv()
            csum[step, :, columns] = (mine + xrecv_buf[step, :, columns].astype(F32)).astype(BF16)
            if step < ndp - 1:
                dp_copy(part, step).start()

    for slot in range(slots):
        @pl.when(head_in_slot(me, slot, n)[1])
        def _():
            await_head(slot, 3)
            key_sum[...] = jnp.zeros_like(key_sum)
            value_sum[...] = jnp.zeros_like(value_sum)

            @pl.loop(0, seq // block)
            def _(index):
                span = pl.ds(pl.multiple_of(index * block, block), block)
                grad = heads_ref[slot, 3, span, :]
                probs = jnp.exp(block_scores(slot, span) - norm_ref[slot, span, :])
                attention = result_ref[slot, 0, span, :]
                grad_dot = jnp.sum(grad.astype(F32) * attention.astype(F32), axis=1, keepdims=True)
                dscore = (probs * (dot_nt(grad, heads_ref[slot, 2]) - grad_dot)).astype(BF16)
                result_ref[slot, 1, span, :] = (dot_nn(dscore, heads_ref[slot, 1]) * scale).astype(BF16)
                key_sum[...] += dot_tn(dscore, heads_ref[slot, 0, span, :])
                value_sum[...] += dot_tn(probs.astype(BF16), grad)

            result_ref[slot, 2] = (key_sum[...] * scale).astype(BF16)
            result_ref[slot, 3] = value_sum[...].astype(BF16)
            for tensor in range(1, 4):
                send_home(slot, tensor)

    @pl.loop(0, width // 512)
    def _(index):
        columns = pl.ds(pl.multiple_of(index * 512, 512), 512)
        attended_ref[:, columns] = dot_nn(att_ref[...], full_ref[:, columns]).astype(BF16)

    my_half = pl.ds(pl.multiple_of(core * half, 16), half)
    their_half = pl.ds(pl.multiple_of((1 - core) * half, 16), half)

    def sum_copy(part):
        return remote(
            hsum.at[:, part_columns(part)], zbuf.at[chip],
            zsend.at[part], zrecv.at[chip], dp, 2 * part + core,
        )

    def spread_copy(part, other):
        landed = final.at[my_half, part_columns(part)]
        return remote(landed, landed, bsend.at[other], brecv.at[part], dp, 2 * other + core)

    def pass_copy(part, span):
        landed = final.at[span, part_columns(part)]
        return remote(landed, landed, fsend.at[part], frecv.at[part], dp, sibling)

    def finish(part):
        @pl.when(chip == part)
        def _():
            total = hsum[:, part_columns(part)].astype(F32)
            for other in range(chips):
                if other != part:
                    landed = zbuf.at[other]
                    remote(landed, landed, zsend.at[0], zrecv.at[other], dp, 2 * other + core).wait_recv()
                    total = total + zbuf[other].astype(F32)
            final[my_half, part_columns(part)] = total.astype(BF16)
            for other in range(chips):
                if other != part:
                    spread_copy(part, other).start()

    for part in range(parts):
        columns = part_columns(part)
        total = csum[ndp - 1, :, columns].astype(F32)
        for step in range(ndp - 1):
            dp_copy(part, step).wait_recv()
            total = total + rbuf[step, :, columns].astype(F32)
        hsum[:, columns] = total.astype(BF16)

        @pl.when(chip != part)
        def _():
            sum_copy(part).start()

        if part:
            finish(part - 1)
    finish(parts - 1)

    for part in range(parts):
        @pl.when(chip != part)
        def _():
            spread_copy(part, part).wait_recv()

        pass_copy(part, my_half).start()
    for part in range(parts):
        pass_copy(part, their_half).wait_recv()
    wg_ref[...] = final[...]

    for tensor in range(1, 4):
        receive_home(tensor)
    for tensor, source in enumerate((q_ref, k_ref, v_ref, grad_ref)):
        for head in range(HEADS):
            send_head(tensor, source, head, False)
    for copy in weight_copies + passes:
        copy.wait_send()
    for slot in range(slots):
        @pl.when(head_in_slot(me, slot, n)[1])
        def _():
            for tensor in range(4):
                for step in range(1, n):
                    home_copy(slot, tensor, step).wait_send()
    for part in range(parts):
        for step in range(ndp):
            pair_copy(part, step).wait_send()
            if step < ndp - 1:
                dp_copy(part, step).wait_send()
        pass_copy(part, my_half).wait_send()

        @pl.when(chip != part)
        def _():
            sum_copy(part).wait_send()

        @pl.when(chip == part)
        def _():
            for other in range(chips):
                if other != part:
                    spread_copy(part, other).wait_send()


def copy_kernel(*refs):
    sources, targets, held = refs[:5], refs[5:10], refs[10:15]
    wide_held, in_sem, out_sem = refs[15:]
    loads = [pltpu.make_async_copy(sources[i], held[i], in_sem.at[i]) for i in range(5)]
    stores = [
        pltpu.make_async_copy(held[i] if i < 4 else wide_held, targets[i], out_sem.at[i]) for i in range(5)
    ]
    for i in (4, 0, 1, 2, 3):
        loads[i].start()
    loads[4].wait()
    wide_held[...] = held[4][...].astype(F32)
    stores[4].start()
    for i in range(4):
        loads[i].wait()
        stores[i].start()
    for store in stores:
        store.wait()


def segment_ids(length_row, row_total):
    order = lax.iota(jnp.int32, length_row.shape[0])
    segment_ends = jnp.sum(jnp.where(order[None, :] <= order[:, None], length_row[None, :], 0), axis=1)
    positions = lax.iota(jnp.int32, row_total)
    return jnp.sum((segment_ends[None, :] <= positions[:, None]).astype(jnp.int32), axis=1)


def vmem(count):
    return [pl.BlockSpec(memory_space=pltpu.VMEM)] * count


def local(queries, keys, values, seg_lengths, out_grad, w_out):
    n, ndp = lax.axis_size("ctx"), lax.axis_size("dp")
    rows, inner = queries.shape[1:]
    width = out_grad.shape[2]
    seq = rows * n
    wrows = w_out.shape[0]
    half = wrows // 2
    slots = -(-HEADS // n)
    parts = math.gcd(n // 2, width // 128)
    wide = width // parts
    shape = jax.ShapeDtypeStruct
    dma = pltpu.SemaphoreType.DMA
    segments = segment_ids(seg_lengths[0], seq)
    out_shape = (
        shape((rows, width), BF16), shape((rows, inner), BF16), shape((rows, inner), BF16),
        shape((rows, inner), BF16), shape((wrows, width), F32),
    )
    outputs = pl.pallas_call(
        functools.partial(whole_kernel, n, ndp, parts, 256),
        out_shape=out_shape[:4] + (shape((wrows, width), BF16),),
        in_specs=vmem(7),
        out_specs=tuple(vmem(5)),
        scratch_shapes=[
            pltpu.VMEM((slots, 4, seq, HD), BF16),
            pltpu.VMEM((inner, width), BF16),
            pltpu.VMEM((rows, inner), BF16),
            pltpu.VMEM((slots, 4, seq, HD), BF16),
            pltpu.VMEM((slots, seq, 1), F32),
            pltpu.VMEM((seq, HD), F32),
            pltpu.VMEM((seq, HD), F32),
            pltpu.VMEM((rows, inner), BF16),
            pltpu.VMEM((inner, rows), BF16),
            pltpu.VMEM((ndp, half, width), BF16),
            pltpu.VMEM((ndp, half, width), BF16),
            pltpu.VMEM((ndp, half, width), BF16),
            pltpu.VMEM((ndp - 1, half, width), BF16),
            pltpu.VMEM((half, width), BF16),
            pltpu.VMEM((n // 2, half, wide), BF16),
            pltpu.VMEM((wrows, width), BF16),
            dma((4, HEADS)), dma((slots, 4)), dma((ndp,)), dma((ndp,)), dma((ndp,)), dma((ndp,)),
            dma((4, slots, n)), dma((4, HEADS)),
            dma((ndp, parts)), dma((ndp, parts)), dma((ndp, parts)), dma((ndp, parts)),
            dma((parts,)), dma((n // 2,)), dma((n // 2,)), dma((parts,)), dma((parts,)), dma((parts,)),
        ],
        compiler_params=pltpu.CompilerParams(
            collective_id=0, has_side_effects=True, vmem_limit_bytes=VMEM_BYTES
        ),
    )(queries[0], keys[0], values[0], out_grad[0], w_out, segments[:, None], segments[None, :])
    anywhere = [pl.BlockSpec(memory_space=pl.ANY)] * 5
    attended, query_grad, key_grad, value_grad, weight_grad = pl.pallas_call(
        copy_kernel,
        out_shape=out_shape,
        in_specs=anywhere,
        out_specs=tuple(anywhere),
        scratch_shapes=[pltpu.VMEM(x.shape, BF16) for x in out_shape]
        + [pltpu.VMEM((wrows, width), F32), dma((5,)), dma((5,))],
        compiler_params=pltpu.CompilerParams(vmem_limit_bytes=VMEM_BYTES),
    )(*outputs)
    return (attended[None], query_grad[None], key_grad[None], value_grad[None], weight_grad)


def solution(mesh):
    in_specs = (
        P("dp", "ctx", None),
        P("dp", "ctx", None),
        P("dp", "ctx", None),
        P("dp", None),
        P("dp", "ctx", None),
        P("dp", None),
    )
    out_specs = (
        P("dp", "ctx", None),
        P("dp", "ctx", None),
        P("dp", "ctx", None),
        P("dp", "ctx", None),
        P("dp", None),
    )
    return jax.shard_map(local, mesh=mesh, in_specs=in_specs, out_specs=out_specs, check_vma=False)
```
